32 devices in a mesh: dp: 8 (over z, core), expert: 4 (over y, x).
Axes of the slice: x: 2, y: 2, z: 4, core: 2. Of those that a mesh axis runs over, the one named last changes fastest.
Arguments:
- tokens: bfloat16 [4096, 2048], P(('dp', 'expert')), may hold values from -6 to 6
- norm_gain: float32 [2048], replicated, may hold values from 0.25 to 1.75
- router_weight: bfloat16 [2048, 64], P('dp'), may hold values from -0.25 to 0.25
- expert_ids: int32 [4096, 8], P(('dp', 'expert')), may hold values from 0 to 63, all different within a row; in each aligned block of 128 rows (0 to 127, 128 to 255, ...) at most 32 rows name the same one
- gate_weight: bfloat16 [4, 2048, 1024], P('expert', 'dp'), may hold values from -0.125 to 0.125
- up_weight: bfloat16 [4, 2048, 1024], P('expert', 'dp'), may hold values from -0.125 to 0.125
- down_weight: bfloat16 [4, 2048, 1024], P('expert', 'dp'), may hold values from -0.1875 to 0.1875
- cotangent: bfloat16 [4096, 2048], P(('dp', 'expert')), may hold values from -6 to 6
Outputs:
- mixed: bfloat16 [4096, 2048], P(('dp', 'expert'))
- d_tokens: bfloat16 [4096, 2048], P(('dp', 'expert'))
- d_gain: float32 [2048], replicated
- d_router: float32 [2048, 64], P('dp')
- d_gate: bfloat16 [4, 2048, 1024], P('expert', 'dp')
- d_up: bfloat16 [4, 2048, 1024], P('expert', 'dp')
- d_down: bfloat16 [4, 2048, 1024], P('expert', 'dp')
The draws below stay inside these ranges and needn't reach their ends.
Inputs may be any that keep to these rules, and one draw needn't show every extreme that they name: `expert_ids`: each row names 8 different experts; in the rows of one device no expert is named more than 32 times.
All inputs are finite; a program needn't handle non-finite values.
Results may differ from the reference program's by a relative error of at most 0.018.
Values may be sent and summed in bfloat16 or wider, within the bound.
A program may use at most 128 MiB of HBM per device.

```python
import math
import jax
import jax.numpy as jnp
import numpy as np
from jax import lax

D = 2048
FF = 1024
EXPERTS_ALL = 64
TOP = 8
TOK_DEV = 128
CAP = 32
EXPERTS = 4
TOKENS = 4096
N_DP = 8
N_EXPERT = 4


def steps_of(stream_key, extent, split, least, high):
    loudness, own = 1.0, jax.random.fold_in(stream_key, 6)
    for dim, blocks in split:
        draws = jnp.exp(jax.random.uniform(jax.random.fold_in(own, dim), (blocks,), jnp.float32, least / len(split), high / len(split)))
        loudness = loudness * jnp.repeat(draws, extent[dim] // blocks).reshape([-1 if axis == dim else 1 for axis in range(len(extent))])
    return loudness


def deal_out(stream_key, own, number, rows, amount, top, reach, skew):
    sequence = jax.random.permutation(stream_key, amount)
    heavy_load, ordinary = load_shares(amount, rows * top, reach, skew, True), load_shares(amount, rows * top, reach, skew, False)
    places = jnp.arange(amount)

    def named(sizes, rotation):
        used = int((sizes > 0).sum())
        fixed = max(1, used // 4)
        passed = fixed + (places - fixed + rotation * (used - fixed)) % max(1, amount - fixed)
        return jnp.zeros((amount,), jnp.int32).at[sequence[jnp.where(places < fixed, places, passed)]].set(jnp.asarray(sizes, jnp.int32))

    sizes = jnp.where(number % 4 == 0, named(heavy_load, number // 4), named(ordinary, number - number // 4 - 1))
    mixed = jax.random.permutation(jax.random.fold_in(own, 3), amount)
    source_of, taker = mixed[0:amount // 2 * 2:2], mixed[1:amount // 2 * 2:2]
    slack = jnp.minimum(sizes[source_of] - 1, reach - sizes[taker]) // 2
    slack = jnp.where((source_of == sequence[0]) | (taker == sequence[0]) | (sizes[taker] == 0), 0, jnp.maximum(slack, 0))
    passed = jax.random.randint(jax.random.fold_in(own, 4), (amount // 2,), 0, 1 << 20) % (slack + 1)
    sizes = sizes.at[source_of].add(-passed).at[taker].add(passed)
    labels = jnp.searchsorted(jnp.cumsum(sizes), jnp.arange(rows * top), side="right").astype(jnp.int32)
    grid = labels.reshape(top, rows).T
    grid = grid[jax.random.permutation(jax.random.fold_in(own, 1), rows)]
    rotation = jax.random.randint(jax.random.fold_in(own, 2), (rows, 1), 0, top)
    return jnp.take_along_axis(grid, (jnp.arange(top)[None, :] + rotation) % top, axis=1)


def load_shares(count, total, limit, lean, full):
    portions = [(1 << 20) // math.isqrt(standing ** lean) + 1 for standing in range(1, count + 1)]
    largest = limit if full else min(limit, max(-(-total // count), total * portions[0] // sum(portions)))
    least = 1 if total - largest >= count - 1 else 0
    holding, rest = [largest] + [least] * (count - 1), total - largest - least * (count - 1)
    while rest > 0:
        candidates = [i for i in range(1, count) if holding[i] < largest] or [i for i in range(1, count) if holding[i] < limit]
        mass, budget = sum([portions[i] for i in candidates]), rest
        for i in candidates:
            more = min(limit - holding[i], max(1, budget * portions[i] // mass), rest)
            holding[i] = holding[i] + more
            rest = rest - more
    return np.array(holding)


def gaussian(rng, extent, scale, limit, pieces=(), held_as=jnp.bfloat16):
    values = scale * jax.random.normal(rng, extent, jnp.float32)
    if pieces:
        values = values * steps_of(rng, extent, pieces, -0.22, 0.18)
    return jnp.clip(values, -limit, limit).astype(held_as)


def setup_inputs(seed: int = 0) -> dict:
    key_of = jax.random.split(jax.random.key(seed), 9)
    tokens = gaussian(key_of[0], (TOKENS, D), 1.0, 6.0, ((0, 32),))
    norm_gain = jnp.clip(1.0 + 0.15 * jax.random.normal(key_of[1], (D,), jnp.float32), 0.25, 1.75)
    router_weight = gaussian(key_of[2], (D, EXPERTS_ALL), (D // 4) ** -0.5, 0.25, ((0, 8),))
    expert_ids_keys = jax.random.split(jax.random.fold_in(key_of[3], 1), TOKENS // TOK_DEV)
    expert_ids_turns = jax.random.permutation(jax.random.fold_in(key_of[3], 3), TOKENS // TOK_DEV)
    expert_ids = jax.vmap(lambda own, number: deal_out(jax.random.fold_in(key_of[3], 2), own, number, TOK_DEV, EXPERTS_ALL, TOP, CAP, 1))(expert_ids_keys, expert_ids_turns).reshape((TOKENS, TOP))
    gate_weight = gaussian(key_of[4], (EXPERTS, D, FF), D ** -0.5, 0.125, ((0, 4), (1, 8)))
    up_weight = gaussian(key_of[5], (EXPERTS, D, FF), D ** -0.5, 0.125, ((0, 4), (1, 8)))
    down_weight = gaussian(key_of[6], (EXPERTS, D, FF), FF ** -0.5, 0.1875, ((0, 4), (1, 8)))
    cotangent = gaussian(key_of[7], (TOKENS, D), 1.0, 6.0, ((0, 32),))
    return {"tokens": tokens, "norm_gain": norm_gain, "router_weight": router_weight, "expert_ids": expert_ids, "gate_weight": gate_weight, "up_weight": up_weight, "down_weight": down_weight, "cotangent": cotangent}


EPSILON = 1e-05
HIGHEST = lax.Precision.HIGHEST

def normalize(inputs, norm_gain):
    meansq = lax.optimization_barrier(jnp.mean(inputs * inputs, axis=-1, keepdims=True))
    return inputs * lax.rsqrt(meansq + EPSILON) * norm_gain

def gate_weights(logits, expert_ids):
    member = (expert_ids[:, :, None] == jnp.arange(logits.shape[-1], dtype=jnp.int32)[None, None, :]).astype(jnp.float32)
    picked = lax.optimization_barrier(jnp.sum(member * logits[:, None, :], axis=-1))
    raised = jnp.exp(picked)
    return raised / lax.optimization_barrier(jnp.sum(raised, axis=-1, keepdims=True))

def pick_matrix(expert_ids, window, capacity):
    flat_ids = expert_ids.reshape(-1).astype(jnp.int32)
    chosen = (flat_ids[:, None] == jnp.arange(window, dtype=jnp.int32)[None, :]).astype(jnp.int32)
    before = (jnp.cumsum(chosen, axis=0, dtype=jnp.int32) - chosen).astype(jnp.int32)
    position = lax.optimization_barrier(jnp.sum(before * chosen, axis=-1)).astype(jnp.int32)
    target = jnp.where(flat_ids < window, flat_ids * capacity + position, -1).astype(jnp.int32)
    columns = jnp.arange(window * capacity, dtype=jnp.int32)
    matrix = (target[:, None] == columns[None, :]).astype(jnp.float32)
    return matrix.reshape(expert_ids.shape[0], expert_ids.shape[1], window * capacity)

def expert_forward(slot_rows, w_gate, w_up, w_down):
    gate_pre = jnp.dot(slot_rows, w_gate, preferred_element_type=jnp.float32)
    up_pre = jnp.dot(slot_rows, w_up, preferred_element_type=jnp.float32)
    active = (gate_pre * jax.nn.sigmoid(gate_pre) * up_pre).astype(jnp.bfloat16)
    output = jnp.dot(active, w_down.T, preferred_element_type=jnp.float32).astype(jnp.bfloat16)
    return (output, gate_pre, up_pre)

def expert_backward(slot_grads, gate_pre, up_pre, w_gate, w_up, w_down):
    sigmoid_gate = jax.nn.sigmoid(gate_pre)
    active = (gate_pre * sigmoid_gate * up_pre).astype(jnp.bfloat16)
    back = jnp.dot(slot_grads, w_down, preferred_element_type=jnp.float32)
    grad_gate = (back * up_pre * sigmoid_gate * (1.0 + gate_pre * (1.0 - sigmoid_gate))).astype(jnp.bfloat16)
    grad_upper = (back * gate_pre * sigmoid_gate).astype(jnp.bfloat16)
    grad_rows = jnp.dot(grad_gate, w_gate.T, preferred_element_type=jnp.float32)
    grad_rows = (grad_rows + jnp.dot(grad_upper, w_up.T, preferred_element_type=jnp.float32)).astype(jnp.bfloat16)
    return (grad_rows, active, grad_gate, grad_upper)

def group_terms(slot_rows, slot_grads, active, grad_gate, grad_upper):
    rows_wide = slot_rows.astype(jnp.float32)
    term_gate = jnp.einsum('krd,krf->kdf', rows_wide, grad_gate.astype(jnp.float32), precision=HIGHEST)
    term_upper = jnp.einsum('krd,krf->kdf', rows_wide, grad_upper.astype(jnp.float32), precision=HIGHEST)
    term_down = jnp.einsum('krd,krf->kdf', slot_grads.astype(jnp.float32), active.astype(jnp.float32), precision=HIGHEST)
    stacked = jnp.concatenate([term_gate, term_upper, term_down], axis=-1)
    rounded = lax.optimization_barrier(stacked.astype(jnp.bfloat16)).astype(jnp.float32)
    return lax.optimization_barrier(jnp.sum(rounded, axis=0))

def reference(tokens, norm_gain, router_weight, expert_ids, gate_weight, up_weight, down_weight, cotangent):
    blocks = N_DP * N_EXPERT
    slot_count = EXPERTS * CAP
    inputs = tokens.astype(jnp.float32)
    hidden = normalize(inputs, norm_gain).astype(jnp.bfloat16)
    logits = jnp.dot(hidden, router_weight, preferred_element_type=jnp.float32)
    weights, gate_back = jax.vjp(lambda values: gate_weights(values, expert_ids), logits)
    pick_table = jax.vmap(lambda block_ids: pick_matrix(block_ids, EXPERTS, CAP))(expert_ids.reshape(blocks, TOK_DEV, TOP))
    spread = lax.optimization_barrier(jnp.sum(pick_table, axis=2))
    blending = jnp.einsum('btks,btk->bts', pick_table, weights.reshape(blocks, TOK_DEV, TOP), precision=HIGHEST)
    hidden_blocks = hidden.reshape(blocks, TOK_DEV, D).astype(jnp.float32)
    cot_blocks = cotangent.reshape(blocks, TOK_DEV, D).astype(jnp.float32)
    outgoing = jnp.einsum('bts,btd->bsd', spread, hidden_blocks, precision=HIGHEST).astype(jnp.bfloat16)
    outgoing_grad = jnp.einsum('bts,btd->bsd', blending, cot_blocks, precision=HIGHEST).astype(jnp.bfloat16)

    def arrange(values):
        shaped = values.reshape(N_DP, N_EXPERT, EXPERTS, CAP, D).transpose(2, 0, 1, 3, 4)
        return shaped.reshape(EXPERTS, N_DP, N_EXPERT * CAP, D)

    def restore(values):
        shaped = values.reshape(EXPERTS, N_DP, N_EXPERT, CAP, D).transpose(1, 2, 0, 3, 4)
        return shaped.reshape(blocks, slot_count, D)

    def one_expert(operands):
        slot_rows, slot_grads, w_gate, w_up, w_down = operands
        flat_rows = slot_rows.reshape(-1, D)
        flat_grads = slot_grads.reshape(-1, D)
        output, gate_pre, up_pre = expert_forward(flat_rows, w_gate, w_up, w_down)
        grad_rows, active, grad_gate, grad_upper = expert_backward(flat_grads, gate_pre, up_pre, w_gate, w_up, w_down)
        summed = group_terms(slot_rows, slot_grads, active.reshape(N_DP, -1, FF), grad_gate.reshape(N_DP, -1, FF), grad_upper.reshape(N_DP, -1, FF))
        return (output.reshape(slot_rows.shape), grad_rows.reshape(slot_rows.shape), summed)
    outputs, grad_slots, weight_grads = lax.map(one_expert, (arrange(outgoing), arrange(outgoing_grad), gate_weight, up_weight, down_weight))
    returned = restore(outputs).astype(jnp.float32)
    returned_grad = restore(grad_slots).astype(jnp.float32)
    mixed_out = jnp.einsum('bts,bsd->btd', blending, returned, precision=HIGHEST).astype(jnp.bfloat16).reshape(-1, D)
    gathered_cot = jnp.einsum('bts,btd->bsd', spread, cot_blocks, precision=HIGHEST)
    per_slot = lax.optimization_barrier(jnp.sum(gathered_cot * returned, axis=-1))
    grad_weights = jnp.einsum('btks,bs->btk', pick_table, per_slot, precision=HIGHEST).reshape(-1, TOP)
    grad_logits = gate_back(grad_weights)[0]
    grad_hidden = jnp.einsum('bts,bsd->btd', spread, returned_grad, precision=HIGHEST).reshape(-1, D)
    grad_hidden = grad_hidden + jnp.dot(grad_logits, router_weight.astype(jnp.float32).T, precision=HIGHEST)
    unused_value, norm_back = jax.vjp(normalize, inputs, norm_gain)
    grad_inputs, grad_gain = norm_back(grad_hidden)
    grad_router = jnp.dot(hidden.astype(jnp.float32).T, grad_logits, precision=HIGHEST)
    grad_gate_out = weight_grads[:, :, :FF].astype(jnp.bfloat16)
    grad_up_out = weight_grads[:, :, FF:2 * FF].astype(jnp.bfloat16)
    grad_down_out = weight_grads[:, :, 2 * FF:].astype(jnp.bfloat16)
    return (mixed_out, grad_inputs.astype(jnp.bfloat16), grad_gain, grad_router, grad_gate_out, grad_up_out, grad_down_out)
```

```python
import jax
import jax.numpy as jnp
from jax import lax
from jax.sharding import PartitionSpec as P

D = 2048
FF = 1024
CAP = 32


EPSILON = 1e-05
HIGHEST = lax.Precision.HIGHEST


def normalize(inputs, norm_gain):
    meansq = jnp.mean(inputs * inputs, axis=-1, keepdims=True)
    return inputs * lax.rsqrt(meansq + EPSILON) * norm_gain


def gate_weights(logits, expert_ids):
    member = (
        expert_ids[:, :, None] == jnp.arange(logits.shape[-1], dtype=jnp.int32)[None, None, :]
    ).astype(jnp.float32)
    picked = jnp.sum(member * logits[:, None, :], axis=-1)
    raised = jnp.exp(picked)
    return raised / jnp.sum(raised, axis=-1, keepdims=True)


def pick_matrix(expert_ids, window, capacity):
    flat_ids = expert_ids.reshape(-1)
    chosen = (flat_ids[:, None] == jnp.arange(window, dtype=jnp.int32)[None, :]).astype(jnp.int32)
    order = jnp.arange(flat_ids.shape[0], dtype=jnp.int32)
    earlier = (order[None, :] < order[:, None]).astype(jnp.bfloat16)
    before = jnp.dot(
        earlier, chosen.astype(jnp.bfloat16), preferred_element_type=jnp.float32
    ).astype(jnp.int32)
    position = jnp.sum(before * chosen, axis=-1)
    target = jnp.where(flat_ids < window, flat_ids * capacity + position, -1)
    columns = jnp.arange(window * capacity, dtype=jnp.int32)
    matrix = (target[:, None] == columns[None, :]).astype(jnp.float32)
    return matrix.reshape(expert_ids.shape[0], expert_ids.shape[1], window * capacity)


def expert_forward(slot_rows, w_gate, w_up, w_down):
    gate_pre = jnp.dot(slot_rows, w_gate, preferred_element_type=jnp.float32)
    up_pre = jnp.dot(slot_rows, w_up, preferred_element_type=jnp.float32)
    active = (gate_pre * jax.nn.sigmoid(gate_pre) * up_pre).astype(jnp.bfloat16)
    output = jnp.dot(active, w_down.T, preferred_element_type=jnp.float32).astype(jnp.bfloat16)
    return (output, gate_pre, up_pre)


def expert_backward(slot_grads, gate_pre, up_pre, w_gate, w_up, w_down):
    sigmoid_gate = jax.nn.sigmoid(gate_pre)
    active = (gate_pre * sigmoid_gate * up_pre).astype(jnp.bfloat16)
    back = jnp.dot(slot_grads, w_down, preferred_element_type=jnp.float32)
    grad_gate = (back * up_pre * sigmoid_gate * (1.0 + gate_pre * (1.0 - sigmoid_gate))).astype(
        jnp.bfloat16
    )
    grad_upper = (back * gate_pre * sigmoid_gate).astype(jnp.bfloat16)
    grad_rows = jnp.dot(grad_gate, w_gate.T, preferred_element_type=jnp.float32)
    grad_rows = (
        grad_rows + jnp.dot(grad_upper, w_up.T, preferred_element_type=jnp.float32)
    ).astype(jnp.bfloat16)
    return (grad_rows, active, grad_gate, grad_upper)


def group_terms(slot_rows, slot_grads, active, grad_gate, grad_upper):
    term_gate = jnp.einsum("krd,krf->kdf", slot_rows, grad_gate, preferred_element_type=jnp.float32)
    term_upper = jnp.einsum(
        "krd,krf->kdf", slot_rows, grad_upper, preferred_element_type=jnp.float32
    )
    term_down = jnp.einsum("krd,krf->kdf", slot_grads, active, preferred_element_type=jnp.float32)
    stacked = jnp.concatenate([term_gate, term_upper, term_down], axis=-1)
    rounded = lax.optimization_barrier(stacked.astype(jnp.bfloat16)).astype(jnp.float32)
    return jnp.sum(rounded, axis=0)


def body(
    tokens, norm_gain, router_weight, expert_ids, gate_weight, up_weight, down_weight, cotangent
):
    window = lax.axis_size("expert")
    groups_dp = lax.axis_size("dp")
    slot_count = window * CAP
    router_full = lax.all_gather(router_weight, "dp", axis=0, tiled=True)
    inputs = tokens.astype(jnp.float32)
    hidden = normalize(inputs, norm_gain).astype(jnp.bfloat16)
    logits = jnp.dot(hidden, router_full, preferred_element_type=jnp.float32)
    weights, gate_back = jax.vjp(lambda values: gate_weights(values, expert_ids), logits)
    pick_table = pick_matrix(expert_ids, window, CAP)
    spread_half = jnp.sum(pick_table, axis=1).astype(jnp.bfloat16)
    blending = jnp.einsum("tks,tk->ts", pick_table, weights, precision=HIGHEST)
    outgoing = (
        jnp.dot(spread_half.T, hidden, preferred_element_type=jnp.float32)
        .astype(jnp.bfloat16)
        .reshape(window, CAP, D)
    )
    weights_full = (
        lax.all_gather(gate_weight, "dp", axis=1, tiled=True),
        lax.all_gather(up_weight, "dp", axis=1, tiled=True),
        lax.all_gather(down_weight, "dp", axis=1, tiled=True),
    )
    w_gate = weights_full[0][0]
    w_up = weights_full[1][0]
    w_down = weights_full[2][0]
    arrived_rows = lax.all_to_all(outgoing, "expert", split_axis=0, concat_axis=0, tiled=True)
    lead = arrived_rows.shape[0]
    middle = arrived_rows.shape[1]
    output, gate_pre, up_pre = expert_forward(arrived_rows.reshape(-1, D), w_gate, w_up, w_down)
    produced = output.reshape(lead, middle, D)
    gate_slots = gate_pre.reshape(lead, middle, FF)
    upper_slots = up_pre.reshape(lead, middle, FF)
    returned = lax.all_to_all(produced, "expert", split_axis=0, concat_axis=0, tiled=True).reshape(
        slot_count, D
    )
    returned_wide = returned.astype(jnp.float32)
    mixed_out = jnp.dot(blending, returned_wide, precision=HIGHEST).astype(jnp.bfloat16)
    gathered_cot = jnp.dot(spread_half.T, cotangent, preferred_element_type=jnp.float32)
    per_slot = jnp.sum(gathered_cot * returned_wide, axis=-1)
    grad_weights = jnp.einsum("tks,s->tk", pick_table, per_slot, precision=HIGHEST)
    grad_logits = gate_back(grad_weights)[0]
    outgoing_grad = (
        jnp.dot(blending.T, cotangent.astype(jnp.float32), precision=HIGHEST)
        .astype(jnp.bfloat16)
        .reshape(window, CAP, D)
    )
    arrived_grad = lax.all_to_all(outgoing_grad, "expert", split_axis=0, concat_axis=0, tiled=True)
    flat_rows = arrived_rows.reshape(-1, D)
    flat_grads = arrived_grad.reshape(-1, D)
    grad_rows, active, grad_gate, grad_upper = expert_backward(
        flat_grads, gate_slots.reshape(-1, FF), upper_slots.reshape(-1, FF), w_gate, w_up, w_down
    )
    grad_back = lax.all_to_all(
        grad_rows.reshape(window, CAP, D), "expert", split_axis=0, concat_axis=0, tiled=True
    ).reshape(slot_count, D)
    shard_rows = D // groups_dp
    rows_cut, grads_cut = (
        lax.all_to_all(flat_rows, "dp", split_axis=1, concat_axis=0, tiled=True),
        lax.all_to_all(flat_grads, "dp", split_axis=1, concat_axis=0, tiled=True),
    )
    per_group = flat_rows.shape[0]
    pieces = (
        lax.all_gather(grad_gate, "dp", axis=0, tiled=True),
        lax.all_gather(grad_upper, "dp", axis=0, tiled=True),
        lax.all_gather(active, "dp", axis=0, tiled=True),
    )
    extent = pieces[0].shape[0]
    groups_in = extent // per_group
    rows_part = rows_cut.reshape(groups_in, per_group, shard_rows)
    grads_part = grads_cut.reshape(groups_in, per_group, shard_rows)
    gate_part = pieces[0].reshape(groups_in, per_group, FF)
    upper_part = pieces[1].reshape(groups_in, per_group, FF)
    active_part = pieces[2].reshape(groups_in, per_group, FF)
    summed = group_terms(rows_part, grads_part, active_part, gate_part, upper_part)
    grad_hidden = jnp.dot(spread_half, grad_back, preferred_element_type=jnp.float32)
    grad_hidden = grad_hidden + jnp.dot(
        grad_logits, router_full.astype(jnp.float32).T, precision=HIGHEST
    )
    unused_value, norm_back = jax.vjp(normalize, inputs, norm_gain)
    grad_inputs, grad_gain = norm_back(grad_hidden)
    grad_router = jnp.dot(hidden.astype(jnp.float32).T, grad_logits, precision=HIGHEST)
    router_part = lax.psum_scatter(
        grad_router.astype(jnp.bfloat16), "dp", scatter_dimension=0, tiled=True
    )
    router_mine = lax.psum(router_part, "expert").astype(jnp.float32)
    gain_sum = lax.psum(grad_gain, ("dp", "expert"))
    grad_gate_out = summed[:, :FF].astype(jnp.bfloat16)[None]
    grad_up_out = summed[:, FF : 2 * FF].astype(jnp.bfloat16)[None]
    grad_down_out = summed[:, 2 * FF :].astype(jnp.bfloat16)[None]
    return (
        mixed_out,
        grad_inputs.astype(jnp.bfloat16),
        gain_sum,
        router_mine,
        grad_gate_out,
        grad_up_out,
        grad_down_out,
    )


def solution(mesh):
    in_specs = (
        P(("dp", "expert"), None),
        P(),
        P("dp", None),
        P(("dp", "expert"), None),
        P("expert", "dp", None),
        P("expert", "dp", None),
        P("expert", "dp", None),
        P(("dp", "expert"), None),
    )
    out_specs = (
        P(("dp", "expert"), None),
        P(("dp", "expert"), None),
        P(),
        P("dp", None),
        P("expert", "dp", None),
        P("expert", "dp", None),
        P("expert", "dp", None),
    )
    return jax.shard_map(body, mesh=mesh, in_specs=in_specs, out_specs=out_specs, check_vma=False)
```

```python
import jax
import jax.numpy as jnp
from jax import lax
from jax.sharding import PartitionSpec as P

D = 2048
FF = 1024
CAP = 32


EPSILON = 1e-05
HIGHEST = lax.Precision.HIGHEST


def normalize(inputs, norm_gain):
    meansq = jnp.mean(inputs * inputs, axis=-1, keepdims=True)
    return inputs * lax.rsqrt(meansq + EPSILON) * norm_gain


def gate_weights(logits, expert_ids):
    member = (
        expert_ids[:, :, None] == jnp.arange(logits.shape[-1], dtype=jnp.int32)[None, None, :]
    ).astype(jnp.float32)
    picked = jnp.sum(member * logits[:, None, :], axis=-1)
    raised = jnp.exp(picked)
    return raised / jnp.sum(raised, axis=-1, keepdims=True)


def pick_matrix(expert_ids, window, capacity):
    flat_ids = expert_ids.reshape(-1)
    chosen = (flat_ids[:, None] == jnp.arange(window, dtype=jnp.int32)[None, :]).astype(jnp.int32)
    order = jnp.arange(flat_ids.shape[0], dtype=jnp.int32)
    earlier = (order[None, :] < order[:, None]).astype(jnp.bfloat16)
    before = jnp.dot(
        earlier, chosen.astype(jnp.bfloat16), preferred_element_type=jnp.float32
    ).astype(jnp.int32)
    position = jnp.sum(before * chosen, axis=-1)
    target = jnp.where(flat_ids < window, flat_ids * capacity + position, -1)
    columns = jnp.arange(window * capacity, dtype=jnp.int32)
    matrix = (target[:, None] == columns[None, :]).astype(jnp.float32)
    return matrix.reshape(expert_ids.shape[0], expert_ids.shape[1], window * capacity)


def small_gather(values, axis):
    count = lax.axis_size(axis)
    copies = jnp.broadcast_to(values[None], (count,) + values.shape)
    return lax.all_to_all(copies, axis, split_axis=0, concat_axis=0, tiled=True)


def expert_pass(slot_rows, slot_grads, w_gate, w_up, w_down):
    gate_pre = jnp.dot(slot_rows, w_gate, preferred_element_type=jnp.float32)
    up_pre = jnp.dot(slot_rows, w_up, preferred_element_type=jnp.float32)
    sigmoid_gate = jax.nn.sigmoid(gate_pre)
    active = (gate_pre * sigmoid_gate * up_pre).astype(jnp.bfloat16)
    back = jnp.dot(slot_grads, w_down, preferred_element_type=jnp.float32)
    grad_gate = (back * up_pre * sigmoid_gate * (1.0 + gate_pre * (1.0 - sigmoid_gate))).astype(
        jnp.bfloat16
    )
    grad_upper = (back * gate_pre * sigmoid_gate).astype(jnp.bfloat16)
    return (active, grad_gate, grad_upper)


def body(
    tokens, norm_gain, router_weight, expert_ids, gate_weight, up_weight, down_weight, cotangent
):
    window = lax.axis_size("expert")
    groups_dp = lax.axis_size("dp")
    slot_count = window * CAP
    shard_rows = D // groups_dp
    w_gate = lax.all_gather(gate_weight[0], "dp", axis=0, tiled=True)
    w_up = lax.all_gather(up_weight[0], "dp", axis=0, tiled=True)
    w_down = lax.all_gather(down_weight[0], "dp", axis=0, tiled=True)
    router_full = small_gather(router_weight, "dp").reshape(D, router_weight.shape[1])
    inputs = tokens.astype(jnp.float32)
    hidden = normalize(inputs, norm_gain).astype(jnp.bfloat16)
    logits = jnp.dot(hidden, router_full, preferred_element_type=jnp.float32)
    weights, gate_back = jax.vjp(lambda values: gate_weights(values, expert_ids), logits)
    pick_table = pick_matrix(expert_ids, window, CAP)
    spread_half = jnp.sum(pick_table, axis=1).astype(jnp.bfloat16)
    blending = jnp.sum(pick_table * weights[:, :, None], axis=1)
    outgoing = jnp.dot(spread_half.T, hidden, preferred_element_type=jnp.float32).astype(
        jnp.bfloat16
    )
    outgoing_grad = jnp.dot(
        blending.T, cotangent.astype(jnp.float32), precision=HIGHEST
    ).astype(jnp.bfloat16)
    leaving = jnp.stack(
        [outgoing.reshape(window, CAP, D), outgoing_grad.reshape(window, CAP, D)], axis=1
    )
    arrived = lax.all_to_all(leaving, "expert", split_axis=0, concat_axis=0, tiled=True)
    flat_rows = arrived[:, 0].reshape(slot_count, D)
    flat_grads = arrived[:, 1].reshape(slot_count, D)
    cut = jnp.stack([flat_rows, flat_grads]).reshape(2, slot_count, groups_dp, shard_rows)
    cut = lax.all_to_all(
        cut.transpose(2, 0, 1, 3), "dp", split_axis=0, concat_axis=0, tiled=True
    )
    rows_cut = cut[:, 0].reshape(groups_dp * slot_count, shard_rows)
    grads_cut = cut[:, 1].reshape(groups_dp * slot_count, shard_rows)
    active, grad_gate, grad_upper = expert_pass(flat_rows, flat_grads, w_gate, w_up, w_down)
    units = lax.all_gather(
        jnp.concatenate([grad_gate, grad_upper, active], axis=1), "dp", axis=0, tiled=True
    )
    output = jnp.dot(active, w_down.T, preferred_element_type=jnp.float32).astype(jnp.bfloat16)
    grad_rows = jnp.dot(grad_gate, w_gate.T, preferred_element_type=jnp.float32)
    grad_rows = (
        grad_rows + jnp.dot(grad_upper, w_up.T, preferred_element_type=jnp.float32)
    ).astype(jnp.bfloat16)
    produced = jnp.stack(
        [output.reshape(window, CAP, D), grad_rows.reshape(window, CAP, D)], axis=1
    )
    came_back = lax.all_to_all(produced, "expert", split_axis=0, concat_axis=0, tiled=True)
    returned = came_back[:, 0].reshape(slot_count, D)
    grad_back = came_back[:, 1].reshape(slot_count, D)
    returned_wide = returned.astype(jnp.float32)
    mixed_out = jnp.dot(blending, returned_wide, precision=HIGHEST).astype(jnp.bfloat16)
    gathered_cot = jnp.dot(spread_half.T, cotangent, preferred_element_type=jnp.float32)
    per_slot = jnp.sum(gathered_cot * returned_wide, axis=-1)
    grad_weights = jnp.sum(pick_table * per_slot[None, None, :], axis=-1)
    grad_logits = gate_back(grad_weights)[0]
    grad_router = jnp.dot(hidden.astype(jnp.float32).T, grad_logits, precision=HIGHEST)
    router_parts = lax.all_to_all(
        grad_router.astype(jnp.bfloat16).reshape(groups_dp, shard_rows, -1),
        "dp",
        split_axis=0,
        concat_axis=0,
        tiled=True,
    )
    router_part = jnp.sum(router_parts.astype(jnp.float32), axis=0)
    router_mine = jnp.sum(small_gather(router_part, "expert"), axis=0)
    grad_hidden = jnp.dot(spread_half, grad_back, preferred_element_type=jnp.float32)
    grad_hidden = grad_hidden + jnp.dot(
        grad_logits, router_full.astype(jnp.float32).T, precision=HIGHEST
    )
    unused_value, norm_back = jax.vjp(normalize, inputs, norm_gain)
    grad_inputs, grad_gain = norm_back(grad_hidden)
    gain_sum = jnp.sum(small_gather(grad_gain, ("dp", "expert")), axis=0)
    grad_rows_pair = lax.dot_general(
        rows_cut,
        units[:, : 2 * FF],
        (((0,), (0,)), ((), ())),
        preferred_element_type=jnp.float32,
    ).astype(jnp.bfloat16)
    grad_down = lax.dot_general(
        grads_cut,
        units[:, 2 * FF :],
        (((0,), (0,)), ((), ())),
        preferred_element_type=jnp.float32,
    ).astype(jnp.bfloat16)
    return (
        mixed_out,
        grad_inputs.astype(jnp.bfloat16),
        gain_sum,
        router_mine,
        grad_rows_pair[:, :FF][None],
        grad_rows_pair[:, FF:][None],
        grad_down[None],
    )


def solution(mesh):
    in_specs = (
        P(("dp", "expert"), None),
        P(),
        P("dp", None),
        P(("dp", "expert"), None),
        P("expert", "dp", None),
        P("expert", "dp", None),
        P("expert", "dp", None),
        P(("dp", "expert"), None),
    )
    out_specs = (
        P(("dp", "expert"), None),
        P(("dp", "expert"), None),
        P(),
        P("dp", None),
        P("expert", "dp", None),
        P("expert", "dp", None),
        P("expert", "dp", None),
    )
    return jax.shard_map(body, mesh=mesh, in_specs=in_specs, out_specs=out_specs, check_vma=False)
```

```python
import jax
import jax.numpy as jnp
from jax import lax
from jax.sharding import PartitionSpec as P

D = 2048
FF = 1024
CAP = 32


EPSILON = 1e-05
HIGHEST = lax.Precision.HIGHEST


def normalize(inputs, norm_gain):
    meansq = jnp.mean(inputs * inputs, axis=-1, keepdims=True)
    return inputs * lax.rsqrt(meansq + EPSILON) * norm_gain


def gate_weights(logits, expert_ids):
    member = (
        expert_ids[:, :, None] == jnp.arange(logits.shape[-1], dtype=jnp.int32)[None, None, :]
    ).astype(jnp.float32)
    picked = jnp.sum(member * logits[:, None, :], axis=-1)
    raised = jnp.exp(picked)
    return raised / jnp.sum(raised, axis=-1, keepdims=True)


def pick_matrix(expert_ids, window, capacity):
    flat_ids = expert_ids.reshape(-1)
    chosen = (flat_ids[:, None] == jnp.arange(window, dtype=jnp.int32)[None, :]).astype(jnp.int32)
    order = jnp.arange(flat_ids.shape[0], dtype=jnp.int32)
    earlier = (order[None, :] < order[:, None]).astype(jnp.bfloat16)
    before = jnp.dot(
        earlier, chosen.astype(jnp.bfloat16), preferred_element_type=jnp.float32
    ).astype(jnp.int32)
    position = jnp.sum(before * chosen, axis=-1)
    target = jnp.where(flat_ids < window, flat_ids * capacity + position, -1)
    columns = jnp.arange(window * capacity, dtype=jnp.int32)
    matrix = (target[:, None] == columns[None, :]).astype(jnp.float32)
    return matrix.reshape(expert_ids.shape[0], expert_ids.shape[1], window * capacity)


def small_gather(values, axis):
    count = lax.axis_size(axis)
    copies = jnp.broadcast_to(values[None], (count,) + values.shape)
    return lax.all_to_all(copies, axis, split_axis=0, concat_axis=0, tiled=True)


def expert_pass(slot_rows, slot_grads, w_gate, w_up, w_down):
    gate_pre = jnp.dot(slot_rows, w_gate, preferred_element_type=jnp.float32)
    up_pre = jnp.dot(slot_rows, w_up, preferred_element_type=jnp.float32)
    sigmoid_gate = jax.nn.sigmoid(gate_pre)
    active = (gate_pre * sigmoid_gate * up_pre).astype(jnp.bfloat16)
    back = jnp.dot(slot_grads, w_down, preferred_element_type=jnp.float32)
    grad_gate = (back * up_pre * sigmoid_gate * (1.0 + gate_pre * (1.0 - sigmoid_gate))).astype(
        jnp.bfloat16
    )
    grad_upper = (back * gate_pre * sigmoid_gate).astype(jnp.bfloat16)
    return (active, grad_gate, grad_upper)


def body(
    tokens, norm_gain, router_weight, expert_ids, gate_weight, up_weight, down_weight, cotangent
):
    window = lax.axis_size("expert")
    groups_dp = lax.axis_size("dp")
    slot_count = window * CAP
    shard_rows = D // groups_dp
    w_gate = lax.all_gather(gate_weight[0], "dp", axis=0, tiled=True)
    w_up = lax.all_gather(up_weight[0], "dp", axis=0, tiled=True)
    w_down = lax.all_gather(down_weight[0], "dp", axis=0, tiled=True)
    router_full = small_gather(router_weight, "dp").reshape(D, router_weight.shape[1])
    inputs = tokens.astype(jnp.float32)
    hidden = normalize(inputs, norm_gain).astype(jnp.bfloat16)
    logits = jnp.dot(hidden, router_full, preferred_element_type=jnp.float32)
    weights, gate_back = jax.vjp(lambda values: gate_weights(values, expert_ids), logits)
    pick_table = pick_matrix(expert_ids, window, CAP)
    spread_half = jnp.sum(pick_table, axis=1).astype(jnp.bfloat16)
    blending = jnp.sum(pick_table * weights[:, :, None], axis=1)
    outgoing = jnp.dot(spread_half.T, hidden, preferred_element_type=jnp.float32).astype(
        jnp.bfloat16
    )
    outgoing_grad = jnp.dot(
        blending.T, cotangent.astype(jnp.float32), precision=HIGHEST
    ).astype(jnp.bfloat16)
    leaving = jnp.stack(
        [outgoing.reshape(window, CAP, D), outgoing_grad.reshape(window, CAP, D)], axis=1
    )
    arrived = lax.all_to_all(leaving, "expert", split_axis=0, concat_axis=0, tiled=True)
    flat_rows = arrived[:, 0].reshape(slot_count, D)
    flat_grads = arrived[:, 1].reshape(slot_count, D)
    cut = jnp.stack([flat_rows, flat_grads]).reshape(2, slot_count, groups_dp, shard_rows)
    cut = lax.all_to_all(
        cut.transpose(2, 0, 1, 3), "dp", split_axis=0, concat_axis=0, tiled=True
    )
    cut, late_grads = lax.optimization_barrier((cut, flat_grads))
    rows_cut = cut[:, 0].reshape(groups_dp * slot_count, shard_rows)
    grads_cut = cut[:, 1].reshape(groups_dp * slot_count, shard_rows)
    active, grad_gate, grad_upper = expert_pass(flat_rows, late_grads, w_gate, w_up, w_down)
    units = lax.all_gather(
        jnp.concatenate([grad_gate, grad_upper, active], axis=1), "dp", axis=0, tiled=True
    )
    output = jnp.dot(active, w_down.T, preferred_element_type=jnp.float32).astype(jnp.bfloat16)
    grad_rows = jnp.dot(grad_gate, w_gate.T, preferred_element_type=jnp.float32)
    grad_rows = (
        grad_rows + jnp.dot(grad_upper, w_up.T, preferred_element_type=jnp.float32)
    ).astype(jnp.bfloat16)
    produced = jnp.stack(
        [output.reshape(window, CAP, D), grad_rows.reshape(window, CAP, D)], axis=1
    )
    came_back = lax.all_to_all(produced, "expert", split_axis=0, concat_axis=0, tiled=True)
    returned = came_back[:, 0].reshape(slot_count, D)
    grad_back = came_back[:, 1].reshape(slot_count, D)
    returned_wide = returned.astype(jnp.float32)
    mixed_out = jnp.dot(blending, returned_wide, precision=HIGHEST).astype(jnp.bfloat16)
    gathered_cot = jnp.dot(spread_half.T, cotangent, preferred_element_type=jnp.float32)
    per_slot = jnp.sum(gathered_cot * returned_wide, axis=-1)
    grad_weights = jnp.sum(pick_table * per_slot[None, None, :], axis=-1)
    grad_logits = gate_back(grad_weights)[0]
    grad_router = jnp.dot(hidden.astype(jnp.float32).T, grad_logits, precision=HIGHEST)
    router_parts = lax.all_to_all(
        grad_router.astype(jnp.bfloat16).reshape(groups_dp, shard_rows, -1),
        "dp",
        split_axis=0,
        concat_axis=0,
        tiled=True,
    )
    router_part = jnp.sum(router_parts.astype(jnp.float32), axis=0)
    router_mine = jnp.sum(small_gather(router_part, "expert"), axis=0)
    grad_hidden = jnp.dot(spread_half, grad_back, preferred_element_type=jnp.float32)
    grad_hidden = grad_hidden + jnp.dot(
        grad_logits, router_full.astype(jnp.float32).T, precision=HIGHEST
    )
    unused_value, norm_back = jax.vjp(normalize, inputs, norm_gain)
    grad_inputs, grad_gain = norm_back(grad_hidden)
    gain_sum = jnp.sum(small_gather(grad_gain, ("dp", "expert")), axis=0)
    grad_rows_pair = lax.dot_general(
        rows_cut,
        units[:, : 2 * FF],
        (((0,), (0,)), ((), ())),
        preferred_element_type=jnp.float32,
    ).astype(jnp.bfloat16)
    grad_down = lax.dot_general(
        grads_cut,
        units[:, 2 * FF :],
        (((0,), (0,)), ((), ())),
        preferred_element_type=jnp.float32,
    ).astype(jnp.bfloat16)
    return (
        mixed_out,
        grad_inputs.astype(jnp.bfloat16),
        gain_sum,
        router_mine,
        grad_rows_pair[:, :FF][None],
        grad_rows_pair[:, FF:][None],
        grad_down[None],
    )


def solution(mesh):
    in_specs = (
        P(("dp", "expert"), None),
        P(),
        P("dp", None),
        P(("dp", "expert"), None),
        P("expert", "dp", None),
        P("expert", "dp", None),
        P("expert", "dp", None),
        P(("dp", "expert"), None),
    )
    out_specs = (
        P(("dp", "expert"), None),
        P(("dp", "expert"), None),
        P(),
        P("dp", None),
        P("expert", "dp", None),
        P("expert", "dp", None),
        P("expert", "dp", None),
    )
    return jax.shard_map(body, mesh=mesh, in_specs=in_specs, out_specs=out_specs, check_vma=False)
```

```python
import jax
import jax.numpy as jnp
from jax import lax
from jax.sharding import PartitionSpec as P

D = 2048
FF = 1024
CAP = 32


EPSILON = 1e-05
HIGHEST = lax.Precision.HIGHEST


def normalize(inputs, norm_gain):
    meansq = jnp.mean(inputs * inputs, axis=-1, keepdims=True)
    return inputs * lax.rsqrt(meansq + EPSILON) * norm_gain


def gate_weights(logits, expert_ids):
    member = (
        expert_ids[:, :, None] == jnp.arange(logits.shape[-1], dtype=jnp.int32)[None, None, :]
    ).astype(jnp.float32)
    picked = jnp.sum(member * logits[:, None, :], axis=-1)
    raised = jnp.exp(picked)
    return raised / jnp.sum(raised, axis=-1, keepdims=True)


def pick_matrix(expert_ids, window, capacity):
    flat_ids = expert_ids.reshape(-1)
    chosen = (flat_ids[:, None] == jnp.arange(window, dtype=jnp.int32)[None, :]).astype(jnp.int32)
    order = jnp.arange(flat_ids.shape[0], dtype=jnp.int32)
    earlier = (order[None, :] < order[:, None]).astype(jnp.bfloat16)
    before = jnp.dot(
        earlier, chosen.astype(jnp.bfloat16), preferred_element_type=jnp.float32
    ).astype(jnp.int32)
    position = jnp.sum(before * chosen, axis=-1)
    target = jnp.where(flat_ids < window, flat_ids * capacity + position, -1)
    columns = jnp.arange(window * capacity, dtype=jnp.int32)
    matrix = (target[:, None] == columns[None, :]).astype(jnp.float32)
    return matrix.reshape(expert_ids.shape[0], expert_ids.shape[1], window * capacity)


def small_gather(values, axis):
    count = lax.axis_size(axis)
    copies = jnp.broadcast_to(values[None], (count,) + values.shape)
    return lax.all_to_all(copies, axis, split_axis=0, concat_axis=0, tiled=True)


def expert_pass(slot_rows, slot_grads, w_gate, w_up, w_down):
    gate_pre = jnp.dot(slot_rows, w_gate, preferred_element_type=jnp.float32)
    up_pre = jnp.dot(slot_rows, w_up, preferred_element_type=jnp.float32)
    sigmoid_gate = jax.nn.sigmoid(gate_pre)
    active = (gate_pre * sigmoid_gate * up_pre).astype(jnp.bfloat16)
    back = jnp.dot(slot_grads, w_down, preferred_element_type=jnp.float32)
    grad_gate = (back * up_pre * sigmoid_gate * (1.0 + gate_pre * (1.0 - sigmoid_gate))).astype(
        jnp.bfloat16
    )
    grad_upper = (back * gate_pre * sigmoid_gate).astype(jnp.bfloat16)
    return (active, grad_gate, grad_upper)


def body(
    tokens, norm_gain, router_weight, expert_ids, gate_weight, up_weight, down_weight, cotangent
):
    window = lax.axis_size("expert")
    groups_dp = lax.axis_size("dp")
    slot_count = window * CAP
    shard_rows = D // groups_dp
    w_gate = lax.all_gather(gate_weight[0], "dp", axis=0, tiled=True)
    w_up = lax.all_gather(up_weight[0], "dp", axis=0, tiled=True)
    w_down = lax.all_gather(down_weight[0], "dp", axis=0, tiled=True)
    router_full = small_gather(router_weight, "dp").reshape(D, router_weight.shape[1])
    inputs = tokens.astype(jnp.float32)
    hidden = normalize(inputs, norm_gain).astype(jnp.bfloat16)
    logits = jnp.dot(hidden, router_full, preferred_element_type=jnp.float32)
    weights, gate_back = jax.vjp(lambda values: gate_weights(values, expert_ids), logits)
    pick_table = pick_matrix(expert_ids, window, CAP)
    spread_half = jnp.sum(pick_table, axis=1).astype(jnp.bfloat16)
    blending = jnp.sum(pick_table * weights[:, :, None], axis=1)
    outgoing = jnp.dot(spread_half.T, hidden, preferred_element_type=jnp.float32).astype(
        jnp.bfloat16
    )
    outgoing_grad = jnp.dot(
        blending.T, cotangent.astype(jnp.float32), precision=HIGHEST
    ).astype(jnp.bfloat16)
    leaving = jnp.stack(
        [outgoing.reshape(window, CAP, D), outgoing_grad.reshape(window, CAP, D)], axis=1
    )
    arrived = lax.all_to_all(leaving, "expert", split_axis=0, concat_axis=0, tiled=True)
    flat_rows = arrived[:, 0].reshape(slot_count, D)
    flat_grads = arrived[:, 1].reshape(slot_count, D)
    cut = jnp.stack([flat_rows, flat_grads]).reshape(2, slot_count, groups_dp, shard_rows)
    cut = lax.all_to_all(
        cut.transpose(2, 0, 1, 3), "dp", split_axis=0, concat_axis=0, tiled=True
    )
    cut, late_grads = lax.optimization_barrier((cut, flat_grads))
    rows_cut = cut[:, 0].reshape(groups_dp * slot_count, shard_rows)
    grads_cut = cut[:, 1].reshape(groups_dp * slot_count, shard_rows)
    active, grad_gate, grad_upper = expert_pass(flat_rows, late_grads, w_gate, w_up, w_down)
    units = lax.all_gather(
        jnp.concatenate([grad_gate, grad_upper, active], axis=1), "dp", axis=0, tiled=True
    )
    output = jnp.dot(active, w_down.T, preferred_element_type=jnp.float32).astype(jnp.bfloat16)
    grad_rows = jnp.dot(grad_gate, w_gate.T, preferred_element_type=jnp.float32)
    grad_rows = (
        grad_rows + jnp.dot(grad_upper, w_up.T, preferred_element_type=jnp.float32)
    ).astype(jnp.bfloat16)
    produced = jnp.stack(
        [output.reshape(window, CAP, D), grad_rows.reshape(window, CAP, D)], axis=1
    )
    came_back = lax.all_to_all(produced, "expert", split_axis=0, concat_axis=0, tiled=True)
    returned = came_back[:, 0].reshape(slot_count, D)
    grad_back = came_back[:, 1].reshape(slot_count, D)
    returned_wide = returned.astype(jnp.float32)
    mixed_out = jnp.dot(blending, returned_wide, precision=HIGHEST).astype(jnp.bfloat16)
    gathered_cot = jnp.dot(spread_half.T, cotangent, preferred_element_type=jnp.float32)
    per_slot = jnp.sum(gathered_cot * returned_wide, axis=-1)
    grad_weights = jnp.sum(pick_table * per_slot[None, None, :], axis=-1)
    grad_logits = gate_back(grad_weights)[0]
    grad_router = jnp.dot(hidden.astype(jnp.float32).T, grad_logits, precision=HIGHEST)
    grad_hidden = jnp.dot(spread_half, grad_back, preferred_element_type=jnp.float32)
    grad_hidden = grad_hidden + jnp.dot(
        grad_logits, router_full.astype(jnp.float32).T, precision=HIGHEST
    )
    unused_value, norm_back = jax.vjp(normalize, inputs, norm_gain)
    grad_inputs, grad_gain = norm_back(grad_hidden)
    scored = grad_router.shape[1]
    gain_rows = D // scored
    gain_high = lax.reduce_precision(grad_gain, 8, 7)
    gain_pair = jnp.concatenate([gain_high, grad_gain - gain_high]).reshape(-1, scored)
    sums = jnp.concatenate(
        [
            grad_router.reshape(groups_dp, shard_rows, scored),
            jnp.broadcast_to(gain_pair[None], (groups_dp,) + gain_pair.shape),
        ],
        axis=1,
    ).astype(jnp.bfloat16)
    sums = lax.all_to_all(sums, "dp", split_axis=0, concat_axis=0, tiled=True)
    part = jnp.sum(sums.astype(jnp.float32), axis=0)
    gain_part = part[shard_rows : shard_rows + gain_rows] + part[shard_rows + gain_rows :]
    part = jnp.concatenate([part[:shard_rows], gain_part], axis=0)
    total = jnp.sum(small_gather(part, "expert"), axis=0)
    router_mine = total[:shard_rows]
    gain_sum = total[shard_rows:].reshape(-1)
    grad_rows_pair = lax.dot_general(
        rows_cut,
        units[:, : 2 * FF],
        (((0,), (0,)), ((), ())),
        preferred_element_type=jnp.float32,
    ).astype(jnp.bfloat16)
    grad_down = lax.dot_general(
        grads_cut,
        units[:, 2 * FF :],
        (((0,), (0,)), ((), ())),
        preferred_element_type=jnp.float32,
    ).astype(jnp.bfloat16)
    return (
        mixed_out,
        grad_inputs.astype(jnp.bfloat16),
        gain_sum,
        router_mine,
        grad_rows_pair[:, :FF][None],
        grad_rows_pair[:, FF:][None],
        grad_down[None],
    )


def solution(mesh):
    in_specs = (
        P(("dp", "expert"), None),
        P(),
        P("dp", None),
        P(("dp", "expert"), None),
        P("expert", "dp", None),
        P("expert", "dp", None),
        P("expert", "dp", None),
        P(("dp", "expert"), None),
    )
    out_specs = (
        P(("dp", "expert"), None),
        P(("dp", "expert"), None),
        P(),
        P("dp", None),
        P("expert", "dp", None),
        P("expert", "dp", None),
        P("expert", "dp", None),
    )
    return jax.shard_map(body, mesh=mesh, in_specs=in_specs, out_specs=out_specs, check_vma=False)
```
